32 devices in a mesh: groups: 1, wide: 32 (over z, y, x, core).
Axes of the slice: x: 2, y: 2, z: 4, core: 2. Of those that a mesh axis runs over, the one named last changes fastest.
Arguments:
- queries: bfloat16 [256, 1152], P('groups'), may hold values from -4 to 4
- patch_keys: bfloat16 [4096, 1152], P(('groups', 'wide')), may hold values from -173 to 173
- patch_values: bfloat16 [4096, 2560], P(('groups', 'wide')), may hold values from -6 to 6
- norm_gain: float32 [2560], replicated, may hold values from 0.1 to 1.9
- route_experts: int32 [512, 6], P(('groups', 'wide')), may hold values from 0 to 15, all different within a row; in each aligned block of 16 rows (0 to 15, 16 to 31, ...) at most 16 rows name the same one
- route_weights: int32 [512, 6], P(('groups', 'wide')), may hold values from 1 to 16
- w_gate: bfloat16 [16384, 2560], P('wide'), may hold values from -0.125 to 0.125
- w_up: bfloat16 [16384, 2560], P('wide'), may hold values from -0.125 to 0.125
- w_down: bfloat16 [16384, 2560], P('wide'), may hold values from -0.1875 to 0.1875
Outputs:
- mixed_rows: bfloat16 [512, 2560], P(('groups', 'wide'))
The draws below stay inside these ranges and needn't reach their ends.
Inputs may be any that keep to these rules, and one draw needn't show every extreme that they name: `route_experts`: each row names 6 different experts. In each aligned block of 16 rows (the rows of one device) no expert is named by more than 16 rows, a bound that some block reaches.
All inputs are finite; a program needn't handle non-finite values.
Results may differ from the reference program's by a relative error of at most 0.02.
Values may be sent and summed in bfloat16 or wider, within the bound.
A program may use at most 128 MiB of HBM per device.

```python
import math
import jax
import jax.numpy as jnp
import numpy as np
from jax import lax

D = 2560
FF = 1024
VIS = 1152
HEADS = 16
HD = 72
QUERIES = 256
TOP = 6
ROWS_DEV = 16
EXPERTS = 16
CAP = 16
IMGS = 2
PATCHES = 2048
TOKENS = 512
N_WIDE = 32


def query_table(key):
    return jnp.clip(jax.random.normal(jax.random.fold_in(key, 11), (QUERIES, VIS), jnp.float32), -4.0, 4.0)


def draw_queries(key, part):
    return query_table(key).astype(jnp.bfloat16)


def draw_patch_keys(key, part):
    total_rows = IMGS * PATCHES
    drawn = jax.random.normal(jax.random.fold_in(key, 23), (total_rows, VIS), jnp.float32)
    return jnp.clip(drawn, -4.0, 4.0).astype(jnp.bfloat16)


def set_ends(entries, own_key, least, top_value):
    spot = [jax.random.randint(jax.random.fold_in(own_key, axis), (), 0, length) for axis, length in enumerate(entries.shape)]
    widest = entries.shape.index(max(entries.shape))
    next_to = spot[:widest] + [(spot[widest] + 1) % entries.shape[widest]] + spot[widest + 1:]
    return entries.at[tuple(spot)].set(least).at[tuple(next_to)].set(top_value)


def levels(stream_key, extent, cuts, least, largest):
    def one(dim, parts):
        heights = jax.random.uniform(jax.random.fold_in(jax.random.fold_in(stream_key, 6), dim), (parts,), jnp.float32, least / len(cuts), largest / len(cuts))
        return jnp.repeat(jnp.exp(heights), extent[dim] // parts).reshape((-1,) + (1,) * (len(extent) - dim - 1))

    level = one(*cuts[0])
    for cut in cuts[1:]:
        level = level * one(*cut)
    return level


def assign_block(own_key, own, number, rows, number_of, top, limit, lean):
    order = jax.random.permutation(own_key, number_of)
    packed, common = portions_of(number_of, rows * top, limit, lean, True), portions_of(number_of, rows * top, limit, lean, False)
    places = jnp.arange(number_of)

    def named(sizes, offset_by):
        used = int((sizes > 0).sum())
        fixed = max(1, used // 4)
        moved = fixed + (places - fixed + offset_by * (used - fixed)) % max(1, number_of - fixed)
        return jnp.zeros((number_of,), jnp.int32).at[order[jnp.where(places < fixed, places, moved)]].set(jnp.asarray(sizes, jnp.int32))

    sizes = jnp.where(number % 4 == 0, named(packed, number // 4), named(common, number - number // 4 - 1))
    mixed = jax.random.permutation(jax.random.fold_in(own, 3), number_of)
    source_of, receiver = mixed[0:number_of // 2 * 2:2], mixed[1:number_of // 2 * 2:2]
    room = jnp.minimum(sizes[source_of] - 1, limit - sizes[receiver]) // 2
    room = jnp.where((source_of == order[0]) | (receiver == order[0]) | (sizes[receiver] == 0), 0, jnp.maximum(room, 0))
    moved = jax.random.randint(jax.random.fold_in(own, 4), (number_of // 2,), 0, 1 << 20) % (room + 1)
    sizes = sizes.at[source_of].add(-moved).at[receiver].add(moved)
    members = jnp.searchsorted(jnp.cumsum(sizes), jnp.arange(rows * top), side="right").astype(jnp.int32)
    grid = members.reshape(top, rows).T
    grid = grid[jax.random.permutation(jax.random.fold_in(own, 1), rows)]
    offset_by = jax.random.randint(jax.random.fold_in(own, 2), (rows, 1), 0, top)
    return jnp.take_along_axis(grid, (jnp.arange(top)[None, :] + offset_by) % top, axis=1)


def portions_of(amount, total, most, lean, full):
    loads = [(1 << 20) // math.isqrt(grade ** lean) + 1 for grade in range(1, amount + 1)]
    largest = most if full else min(most, max(-(-total // amount), total * loads[0] // sum(loads)))
    least = 1 if total - largest >= amount - 1 else 0
    counts, surplus = [largest] + [least] * (amount - 1), total - largest - least * (amount - 1)
    while surplus > 0:
        movable = [i for i in range(1, amount) if counts[i] < largest] or [i for i in range(1, amount) if counts[i] < most]
        whole, budget = sum([loads[i] for i in movable]), surplus
        for i in movable:
            more = min(most - counts[i], max(1, budget * loads[i] // whole), surplus)
            counts[i] = counts[i] + more
            surplus = surplus - more
    return np.array(counts)


def gaussian(stream_key, dims, deviation, most, shards=(), held_as=jnp.bfloat16):
    gain = levels(stream_key, dims, shards, -0.22, 0.18) if shards else 1.0
    drawn = jax.random.normal(stream_key, dims, jnp.float32) * deviation * gain
    return jnp.minimum(jnp.maximum(drawn, -most), most).astype(held_as)


def setup_inputs(seed: int = 0, part: int = 0) -> dict:
    arg_keys = jax.random.split(jax.random.key(seed), 10)
    part_splits = jax.random.split(jax.random.fold_in(arg_keys[9], part), 10)
    queries = draw_queries(jax.random.fold_in(jax.random.fold_in(arg_keys[9], part), 71), part)
    patch_keys = draw_patch_keys(jax.random.fold_in(jax.random.fold_in(arg_keys[9], part), 71), part)
    patch_values = gaussian(part_splits[2], (IMGS * PATCHES, D), 1.0, 6.0, ((0, 32),))
    norm_gain = jnp.clip(1.0 + 0.18 * jax.random.normal(arg_keys[3], (D,), jnp.float32), 0.1, 1.9)
    route_experts_keys = jax.random.split(jax.random.fold_in(part_splits[4], 1), TOKENS // ROWS_DEV)
    route_experts_turns = jax.random.permutation(jax.random.fold_in(part_splits[4], 3), TOKENS // ROWS_DEV)
    route_experts = jax.vmap(lambda own, number: assign_block(jax.random.fold_in(part_splits[4], 2), own, number, ROWS_DEV, EXPERTS, TOP, CAP, 2))(route_experts_keys, route_experts_turns).reshape((TOKENS, TOP))
    route_weights = set_ends(jax.random.randint(part_splits[5], (TOKENS, TOP), 1, 17), jax.random.fold_in(part_splits[5], 1), 1, 16).astype(jnp.int32)
    w_gate = gaussian(arg_keys[6], (EXPERTS * FF, D), D ** -0.5, 0.125, ((0, 32),))
    w_up = gaussian(arg_keys[7], (EXPERTS * FF, D), D ** -0.5, 0.125, ((0, 32),))
    w_down = gaussian(arg_keys[8], (EXPERTS * FF, D), FF ** -0.5, 0.1875, ((0, 32),))
    return dict(queries=queries, patch_keys=patch_keys, patch_values=patch_values, norm_gain=norm_gain, route_experts=route_experts, route_weights=route_weights, w_gate=w_gate, w_up=w_up, w_down=w_down)


precise = lax.Precision.HIGHEST

def reference(queries, patch_keys, patch_values, norm_gain, route_experts, route_weights, w_gate, w_up, w_down):
    value_size = D // HEADS
    score_scale = HD ** (-0.5)
    query_heads = queries.astype(jnp.float32).reshape(QUERIES, HEADS, HD)
    key_blocks = patch_keys.reshape(IMGS, PATCHES, HEADS, HD)
    value_blocks = patch_values.reshape(IMGS, PATCHES, HEADS, value_size)

    def attend(key_value):
        key_block, value_block = key_value
        scores = jnp.einsum('qhc,phc->qhp', query_heads, key_block.astype(jnp.float32), precision=precise) * score_scale
        row_peak = lax.optimization_barrier(jnp.max(scores, axis=2, keepdims=True))
        raised = jnp.exp(scores - row_peak)
        row_total = lax.optimization_barrier(jnp.sum(raised, axis=2))
        rounded = lax.optimization_barrier(raised.astype(jnp.bfloat16))
        attended = jnp.einsum('qhp,phc->qhc', rounded.astype(jnp.float32), value_block.astype(jnp.float32), precision=precise)
        attended = attended / row_total[:, :, None]
        return attended.reshape(QUERIES, D).astype(jnp.bfloat16)
    projected = lax.map(attend, (key_blocks, value_blocks)).reshape(TOKENS, D)
    residual = projected.astype(jnp.float32)
    normed = (residual * lax.rsqrt(lax.optimization_barrier(jnp.mean(residual * residual, axis=1, keepdims=True)) + 1e-06) * norm_gain).astype(jnp.bfloat16)
    blocks = route_experts.reshape(N_WIDE, ROWS_DEV * TOP)
    onehot = (blocks[:, :, None] == jnp.arange(EXPERTS, dtype=jnp.int32)[None, None, :]).astype(jnp.int32)
    earlier = jnp.cumsum(onehot, axis=1) - onehot
    slot_index = lax.optimization_barrier(jnp.sum(earlier * onehot, axis=2)).astype(jnp.int32)
    place = (jnp.arange(N_WIDE, dtype=jnp.int32)[:, None] * CAP + slot_index).reshape(-1).astype(jnp.int32)
    expert_id = route_experts.reshape(-1).astype(jnp.int32)
    row_id = (jnp.arange(TOKENS * TOP, dtype=jnp.int32) // TOP).astype(jnp.int32)
    scores_int = route_weights.astype(jnp.float32)
    gate_share = (scores_int / lax.optimization_barrier(jnp.sum(scores_int, axis=1, keepdims=True))).reshape(-1)
    row_table = jnp.zeros((EXPERTS, N_WIDE * CAP), jnp.int32).at[expert_id, place].set(row_id)
    gate_table = jnp.zeros((EXPERTS, N_WIDE * CAP), jnp.float32).at[expert_id, place].set(gate_share)
    gate_blocks = w_gate.reshape(EXPERTS, FF, D)
    up_blocks = w_up.reshape(EXPERTS, FF, D)
    down_blocks = w_down.reshape(EXPERTS, FF, D)

    def expert_step(combined, expert_item):
        table_row, gate_row, gate_matrix, up_matrix, down_matrix = expert_item
        rows_in = normed[table_row]
        gate_part = jnp.dot(rows_in, gate_matrix.T, preferred_element_type=jnp.float32)
        up_part = jnp.dot(rows_in, up_matrix.T, preferred_element_type=jnp.float32)
        hidden = (jax.nn.silu(gate_part) * up_part).astype(jnp.bfloat16)
        expert_out = jnp.dot(hidden, down_matrix, preferred_element_type=jnp.float32).astype(jnp.bfloat16)
        expert_out = lax.optimization_barrier(expert_out)
        combined = combined.at[table_row].add(gate_row[:, None] * expert_out.astype(jnp.float32))
        return (combined, None)
    combined, _ = lax.scan(expert_step, jnp.zeros((TOKENS, D), jnp.float32), (row_table, gate_table, gate_blocks, up_blocks, down_blocks))
    return (residual + combined).astype(jnp.bfloat16)
```

```python
import functools

import jax
import jax.numpy as jnp
from jax import lax
from jax.experimental import pallas as pl
from jax.experimental.pallas import tpu as pltpu
from jax.sharding import PartitionSpec as P

HEADS = 16
LANES = 128
F32 = jnp.float32
BF16 = jnp.bfloat16


def kernel(
    devices,
    q_ref, k_ref, v_ref, gain_ref, re_ref, rw_ref, wg_hbm, wu_hbm, wd_hbm,
    out_ref,
    kvp, kvr, s_scr, p_scr, tot_scr, gath, proj, own_rows, gates, wg, wu, wd,
    pa, pb, r1a, r1b, r2a, r2b, r3a, r3b, ua, ub, r4a, r4b,
    w_sem, a_send, a_recv, g_send, g_recv,
    s1_send, s1_recv, s2_send, s2_recv, s3_send, s3_recv, s4_send, s4_recv,
):
    me = lax.axis_index("wide")
    group = HEADS
    spot = lax.rem(me, group)
    base = me - spot
    depth = devices // 8
    core = lax.rem(me, 2)
    xi = lax.rem(me // 2, 2)
    yi = lax.rem(me // 4, 2)
    zi = me // 8
    n_q = q_ref.shape[0]
    width = v_ref.shape[1]
    patches = k_ref.shape[0]
    key_size = k_ref.shape[1] // HEADS
    value_size = width // HEADS
    extra = value_size - LANES
    pieces = LANES // extra
    half_w = width // 2
    rows_dev = re_ref.shape[0]
    wide_kv = kvp.shape[2]

    def dev(z, y, x, c):
        return z * 8 + y * 4 + x * 2 + c

    sib = dev(zi, yi, xi, 1 - core)
    xn = dev(zi, yi, 1 - xi, core)
    yn = dev(zi, 1 - yi, xi, core)

    def rcopy(src, dst, ssem, rsem, target):
        return pltpu.make_async_remote_copy(
            src_ref=src, dst_ref=dst, send_sem=ssem, recv_sem=rsem,
            device_id={"wide": target}, device_id_type=pl.DeviceIdType.MESH,
        )

    barrier = pltpu.get_barrier_semaphore()
    per_group = group // 8
    for k in range(1, group):
        pl.semaphore_signal(
            barrier, inc=1, device_id={"wide": base + lax.rem(spot + k, group)},
            device_id_type=pl.DeviceIdType.MESH,
        )
    far = depth - per_group
    z_base = zi // per_group * per_group
    for k in range(far):
        zt = lax.rem(z_base + per_group + k, depth)
        pl.semaphore_signal(
            barrier, inc=1, device_id={"wide": dev(zt, yi, xi, core)},
            device_id_type=pl.DeviceIdType.MESH,
        )

    w_copies = [
        pltpu.make_async_copy(wg_hbm, wg, w_sem.at[0]),
        pltpu.make_async_copy(wu_hbm, wu, w_sem.at[1]),
        pltpu.make_async_copy(wd_hbm, wd, w_sem.at[2]),
    ]

    pad = jnp.zeros((patches, wide_kv - value_size - key_size), BF16)
    for h in range(HEADS):
        kvp[h] = jnp.concatenate(
            [
                v_ref[:, h * value_size : (h + 1) * value_size],
                k_ref[:, h * key_size : (h + 1) * key_size],
                pad,
            ],
            axis=1,
        )
    pl.semaphore_wait(barrier, group - 1 + far)

    def a2a(k):
        t = lax.rem(spot + k, group)
        return rcopy(kvp.at[t], kvr.at[spot], a_send.at[k], a_recv.at[k], base + t)

    def a2a_in(k):
        s = lax.rem(spot + group - k, group)
        return rcopy(kvp.at[s], kvr.at[s], a_send.at[k], a_recv.at[k], base + s)

    def send_kv(k, carry):
        a2a(k).start()
        return carry

    lax.fori_loop(1, group, send_kv, 0)
    for c in w_copies:
        c.start()
    kvr[spot] = kvp[spot]

    q_head = jnp.zeros((n_q, key_size), F32)
    for h in range(HEADS):
        q_head = jnp.where(
            spot == h, q_ref[:, h * key_size : (h + 1) * key_size].astype(F32), q_head
        )
    q_pad = jnp.concatenate(
        [
            jnp.zeros((n_q, value_size), F32),
            q_head,
            jnp.zeros((n_q, wide_kv - value_size - key_size), F32),
        ],
        axis=1,
    ).astype(BF16)

    shares = rw_ref[...].astype(F32)
    shares = shares / jnp.sum(shares, axis=1, keepdims=True)
    lane = lax.broadcasted_iota(jnp.int32, (rows_dev, LANES), 1)
    table = jnp.zeros((rows_dev, LANES), F32)
    for k in range(re_ref.shape[1]):
        table = table + jnp.where(re_ref[:, k : k + 1] == lane, shares[:, k : k + 1], 0.0)
    table_hi = table.astype(BF16)
    table_lo = (table - table_hi.astype(F32)).astype(BF16)

    def wait_kv(k, carry):
        a2a_in(k).wait_recv()
        return carry

    lax.fori_loop(1, group, wait_kv, 0)

    scale = key_size ** (-0.5)
    for s in range(group):
        s_scr[:, s * patches : (s + 1) * patches] = (
            lax.dot_general(
                q_pad, kvr[s], (((1,), (1,)), ((), ())), preferred_element_type=F32
            )
            * scale
        )

    step = 32

    def soft(r, carry):
        rows = pl.ds(pl.multiple_of(r * step, step), step)
        s = s_scr[rows, :]
        p = jnp.exp(s - jnp.max(s, axis=1, keepdims=True))
        tot_scr[rows, :] = jnp.broadcast_to(jnp.sum(p, axis=1, keepdims=True), (step, LANES))
        p_scr[rows, :] = p.astype(BF16)
        return carry

    lax.fori_loop(0, n_q // step, soft, 0)
    acc = jnp.zeros((n_q, wide_kv), F32)
    for s in range(group):
        acc = acc + jnp.dot(
            p_scr[:, s * patches : (s + 1) * patches], kvr[s], preferred_element_type=F32
        )
    att = (acc / tot_scr[:, 0:1]).astype(BF16)
    main = n_q
    part = n_q // pieces
    gath[me, 0:main, :] = att[:, :LANES]
    gath[me, main : main + part, :] = jnp.concatenate(
        [att[g * part : (g + 1) * part, LANES : LANES + extra] for g in range(pieces)], axis=1
    )
    gath[me, main + part : main + part + rows_dev, :] = table_hi
    gath[me, main + part + rows_dev : main + part + 2 * rows_dev, :] = table_lo

    tall = main + part + 2 * rows_dev
    half = tall // 2
    top, low = pl.ds(0, half), pl.ds(half, half)

    def src_z(dz):
        return lax.rem(zi + depth - dz, depth)

    def own(dz):
        return dev(src_z(dz), yi, xi, core)

    def blk_x(dz):
        return dev(src_z(dz), yi, 1 - xi, core)

    def blk_y(dz):
        return dev(src_z(dz), 1 - yi, xi, core)

    def blk_d(dz):
        return dev(src_z(dz), 1 - yi, 1 - xi, core)

    def gcopy(kind, dz, block, target, rows=None):
        ref = gath.at[block] if rows is None else gath.at[block, rows]
        return rcopy(ref, ref, g_send.at[kind, dz], g_recv.at[kind, dz], target)

    def z_out(dz):
        zt = lax.rem(zi + dz, depth)
        return gcopy(0, dz, me, dev(zt, yi, xi, core))

    def send_z(dz, carry):
        z_out(dz).start()
        return carry

    lax.fori_loop(1, depth, send_z, 0)

    def spread(dz):
        gcopy(1, dz, own(dz), xn).start()
        gcopy(2, dz, own(dz), yn).start()
        gcopy(3, dz, own(dz), sib).start()

    spread(0)

    def spread_z(dz, carry):
        gcopy(0, dz, own(dz), me).wait_recv()
        spread(dz)
        return carry

    lax.fori_loop(1, depth, spread_z, 0)

    def onward(dz, carry):
        gcopy(1, dz, blk_x(dz), xn).wait_recv()
        gcopy(4, dz, blk_x(dz), yn, top).start()
        gcopy(5, dz, blk_x(dz), sib).start()
        gcopy(2, dz, blk_y(dz), yn).wait_recv()
        gcopy(6, dz, blk_y(dz), xn, low).start()
        gcopy(7, dz, blk_y(dz), sib).start()
        return carry

    lax.fori_loop(0, depth, onward, 0)

    def last(dz, carry):
        gcopy(4, dz, blk_d(dz), yn, top).wait_recv()
        gcopy(6, dz, blk_d(dz), xn, low).wait_recv()
        gcopy(8, dz, blk_d(dz), sib).start()
        return carry

    lax.fori_loop(0, depth, last, 0)

    def other(block):
        return block + 1 - 2 * core

    def from_sib(dz, carry):
        gcopy(3, dz, other(own(dz)), sib).wait_recv()
        gcopy(5, dz, other(blk_x(dz)), sib).wait_recv()
        gcopy(7, dz, other(blk_y(dz)), sib).wait_recv()
        gcopy(8, dz, other(blk_d(dz)), sib).wait_recv()
        return carry

    lax.fori_loop(0, depth, from_sib, 0)

    images = devices // group
    quads = HEADS // pieces

    def lay(it, carry):
        image, quad = it // quads, lax.rem(it, quads)
        first = image * group + quad * pieces
        cols = []
        for g in range(pieces):
            tail = gath[first + g, main : main + part, :]
            cols.append(gath[first + g, 0:main, :])
            cols.append(
                jnp.concatenate(
                    [tail[:, i * extra : (i + 1) * extra] for i in range(pieces)], axis=0
                )
            )
        span = pieces * value_size
        proj[
            pl.ds(pl.multiple_of(image * n_q, n_q), n_q),
            pl.ds(pl.multiple_of(quad * span, LANES), span),
        ] = jnp.concatenate(cols, axis=1)
        return carry

    lax.fori_loop(0, images * quads, lay, 0)

    own_rows[...] = proj[pl.ds(pl.multiple_of(me * rows_dev, rows_dev), rows_dev), :]
    expert = me // 2
    lane_row = lax.broadcasted_iota(jnp.int32, (rows_dev, LANES), 1)

    def norm_rows(d, carry):
        rows = pl.ds(pl.multiple_of(d * rows_dev, rows_dev), rows_dev)
        x = proj[rows, :].astype(F32)
        r = lax.rsqrt(jnp.mean(x * x, axis=1, keepdims=True) + 1e-06)
        proj[rows, :] = (x * r * gain_ref[...]).astype(BF16)
        share = gath[d, main + part : main + part + rows_dev, :].astype(F32) + gath[
            d, main + part + rows_dev : main + part + 2 * rows_dev, :
        ].astype(F32)
        mine = jnp.sum(jnp.where(lane_row == expert, share, 0.0), axis=1, keepdims=True)
        gates[rows, :] = jnp.broadcast_to(mine, (rows_dev, LANES))
        return carry

    lax.fori_loop(0, devices, norm_rows, 0)
    for c in w_copies:
        c.wait()

    block_rows = n_q
    z_block = block_rows // (8 * rows_dev)

    def s1(z, side):
        src = pa if side == 0 else pb
        dst = r1a if side == 0 else r1b
        return rcopy(
            src.at[1 - core, :, z], dst.at[:, z], s1_send.at[side, z], s1_recv.at[side, z], sib
        )

    def experts(r, carry):
        rows = pl.ds(pl.multiple_of(r * block_rows, block_rows), block_rows)
        x = proj[rows, :]
        dims = (((1,), (1,)), ((), ()))
        g = lax.dot_general(x, wg[...], dims, preferred_element_type=F32)
        u = lax.dot_general(x, wu[...], dims, preferred_element_type=F32)
        hidden = (g / (1.0 + jnp.exp(-g)) * u).astype(BF16)
        share = gates[rows, 0:1]
        chunk = half_w // 2
        for n in range(4):
            y = jnp.dot(
                hidden, wd[:, n * chunk : (n + 1) * chunk], preferred_element_type=F32
            )
            y = (y * share).astype(BF16)
            cols = slice((n % 2) * chunk, (n % 2 + 1) * chunk)
            for j in range(8 * z_block):
                c, x_, y_, z = j % 2, j // 2 % 2, j // 4 % 2, j // 8
                piece = y[j * rows_dev : (j + 1) * rows_dev]
                if n < 2:
                    pa[c, x_, r * z_block + z, y_, :, cols] = piece
                else:
                    pb[c, y_, r * z_block + z, x_, :, cols] = piece
        for z in range(z_block):
            s1(r * z_block + z, 0).start()
            s1(r * z_block + z, 1).start()
        return carry

    lax.fori_loop(0, devices * rows_dev // block_rows, experts, 0)

    def add_into(dst, d_ix, others):
        total = dst[d_ix].astype(F32)
        for ref, ix in others:
            total = total + ref[ix].astype(F32)
        return total.astype(BF16)

    def s2a(z):
        return rcopy(pa.at[core, 1 - xi, z], r2a.at[z], s2_send.at[0, z], s2_recv.at[0, z], xn)

    def s2b(z):
        return rcopy(pb.at[core, 1 - yi, z], r2b.at[z], s2_send.at[1, z], s2_recv.at[1, z], yn)

    def home1(z, carry):
        s1(z, 0).wait_recv()
        pa[core, 1 - xi, z] = add_into(pa, (core, 1 - xi, z), [(r1a, (1 - xi, z))])
        s2a(z).start()
        s1(z, 1).wait_recv()
        pb[core, 1 - yi, z] = add_into(pb, (core, 1 - yi, z), [(r1b, (1 - yi, z))])
        s2b(z).start()
        return carry

    lax.fori_loop(0, depth, home1, 0)

    def s3a(z):
        return rcopy(
            pa.at[core, xi, z, 1 - yi], r3a.at[z], s3_send.at[0, z], s3_recv.at[0, z], yn
        )

    def s3b(z):
        return rcopy(
            pb.at[core, yi, z, 1 - xi], r3b.at[z], s3_send.at[1, z], s3_recv.at[1, z], xn
        )

    def home2(z, carry):
        s2a(z).wait_recv()
        pa[core, xi, z] = add_into(pa, (core, xi, z), [(r1a, (xi, z)), (r2a, z)])
        s3a(z).start()
        s2b(z).wait_recv()
        pb[core, yi, z] = add_into(pb, (core, yi, z), [(r1b, (yi, z)), (r2b, z)])
        s3b(z).start()
        return carry

    lax.fori_loop(0, depth, home2, 0)

    def s4(dz, side):
        zt = lax.rem(zi + dz, depth)
        src = ua if side == 0 else ub
        dst = r4a if side == 0 else r4b
        return rcopy(
            src.at[zt], dst.at[dz], s4_send.at[side, dz], s4_recv.at[side, dz],
            dev(zt, yi, xi, core),
        )

    def home3(dz, carry):
        z = lax.rem(zi + dz, depth)
        s3a(z).wait_recv()
        ua[z] = add_into(pa, (core, xi, z, yi), [(r3a, z)])
        s3b(z).wait_recv()
        ub[z] = add_into(pb, (core, yi, z, xi), [(r3b, z)])

        @pl.when(dz > 0)
        def _():
            s4(dz, 0).start()
            s4(dz, 1).start()

        return carry

    def far_first(i, carry):
        return home3(depth - 1 - i, carry)

    lax.fori_loop(0, depth, far_first, 0)
    mine = own_rows[...].astype(F32)
    sum_a = mine[:, :half_w] + ua[zi].astype(F32)
    sum_b = mine[:, half_w:] + ub[zi].astype(F32)

    def home4(dz, carry):
        left, right = carry
        s4(dz, 0).wait_recv()
        s4(dz, 1).wait_recv()
        return left + r4a[dz].astype(F32), right + r4b[dz].astype(F32)

    sum_a, sum_b = lax.fori_loop(1, depth, home4, (sum_a, sum_b))
    out_ref[:, :half_w] = sum_a.astype(BF16)
    out_ref[:, half_w:] = sum_b.astype(BF16)

    def sent_kv(k, carry):
        a2a(k).wait_send()
        return carry

    lax.fori_loop(1, group, sent_kv, 0)

    def sent_z(dz, carry):
        z_out(dz).wait_send()
        s4(dz, 0).wait_send()
        s4(dz, 1).wait_send()
        return carry

    lax.fori_loop(1, depth, sent_z, 0)

    def sent(dz, carry):
        gcopy(1, dz, own(dz), xn).wait_send()
        gcopy(2, dz, own(dz), yn).wait_send()
        gcopy(3, dz, own(dz), sib).wait_send()
        gcopy(4, dz, blk_x(dz), yn, top).wait_send()
        gcopy(5, dz, blk_x(dz), sib).wait_send()
        gcopy(6, dz, blk_y(dz), xn, low).wait_send()
        gcopy(7, dz, blk_y(dz), sib).wait_send()
        gcopy(8, dz, blk_d(dz), sib).wait_send()
        for copy in (s1(dz, 0), s1(dz, 1), s2a(dz), s2b(dz), s3a(dz), s3b(dz)):
            copy.wait_send()
        return carry

    lax.fori_loop(0, depth, sent, 0)


def on_device(
    queries, patch_keys, patch_values, norm_gain, route_experts, route_weights, w_gate, w_up, w_down
):
    devices = lax.axis_size("wide")
    n_q = queries.shape[0]
    patches, vision = patch_keys.shape
    width = patch_values.shape[1]
    rows_dev = route_experts.shape[0]
    hidden = w_gate.shape[0]
    depth = devices // 8
    group = HEADS
    assert n_q == rows_dev * group and n_q % (8 * rows_dev) == 0 and depth % 2 == 0
    value_size = width // HEADS
    extra = value_size - LANES
    pieces = LANES // extra
    wide_kv = -(-(value_size + vision // HEADS) // LANES) * LANES
    tall = n_q + n_q // pieces + 2 * rows_dev
    rows = devices * rows_dev
    half = width // 2
    vm = pltpu.VMEM
    dma = pltpu.SemaphoreType.DMA
    scratch = [
        vm((group, patches, wide_kv), BF16),
        vm((group, patches, wide_kv), BF16),
        vm((n_q, group * patches), F32),
        vm((n_q, group * patches), BF16),
        vm((n_q, LANES), F32),
        vm((devices, tall, LANES), BF16),
        vm((rows, width), BF16),
        vm((rows_dev, width), BF16),
        vm((rows, LANES), F32),
        vm((hidden, width), BF16),
        vm((hidden, width), BF16),
        vm((hidden, width), BF16),
        vm((2, 2, depth, 2, rows_dev, half), BF16),
        vm((2, 2, depth, 2, rows_dev, half), BF16),
        vm((2, depth, 2, rows_dev, half), BF16),
        vm((2, depth, 2, rows_dev, half), BF16),
        vm((depth, 2, rows_dev, half), BF16),
        vm((depth, 2, rows_dev, half), BF16),
        vm((depth, rows_dev, half), BF16),
        vm((depth, rows_dev, half), BF16),
        vm((depth, rows_dev, half), BF16),
        vm((depth, rows_dev, half), BF16),
        vm((depth, rows_dev, half), BF16),
        vm((depth, rows_dev, half), BF16),
        dma((3,)),
        dma((group,)), dma((group,)),
        dma((9, depth)), dma((9, depth)),
        dma((2, depth)), dma((2, depth)),
        dma((2, depth)), dma((2, depth)),
        dma((2, depth)), dma((2, depth)),
        dma((2, depth)), dma((2, depth)),
    ]
    vspec = pl.BlockSpec(memory_space=pltpu.VMEM)
    hspec = pl.BlockSpec(memory_space=pl.ANY)
    return pl.pallas_call(
        functools.partial(kernel, devices),
        out_shape=jax.ShapeDtypeStruct((rows_dev, width), BF16),
        in_specs=[vspec] * 6 + [hspec] * 3,
        out_specs=vspec,
        scratch_shapes=scratch,
        compiler_params=pltpu.CompilerParams(
            collective_id=0, has_side_effects=True, vmem_limit_bytes=62 * 1024 * 1024
        ),
    )(
        queries, patch_keys, patch_values, norm_gain.reshape(1, -1), route_experts, route_weights,
        w_gate, w_up, w_down,
    )


def solution(mesh):
    rows = P(("groups", "wide"), None)
    return jax.shard_map(
        on_device,
        mesh=mesh,
        in_specs=(
            P("groups", None), rows, rows, P(), rows, rows,
            P("wide", None), P("wide", None), P("wide", None),
        ),
        out_specs=rows,
        check_vma=False,
    )
```

```python
import functools

import jax
import jax.numpy as jnp
from jax import lax
from jax.experimental import pallas as pl
from jax.experimental.pallas import tpu as pltpu
from jax.sharding import PartitionSpec as P

HEADS = 16
LANES = 128
F32 = jnp.float32
BF16 = jnp.bfloat16


def kernel(
    devices,
    q_hbm, k_hbm, v_hbm, gain_ref, re_ref, rw_ref, wg_hbm, wu_hbm, wd_hbm,
    out_ref,
    q_ref, k_ref, v_ref, kvp, kvr, s_scr, p_scr, tot_scr, gath, proj, own_rows, gates, wg, wu, wd,
    pa, pb, r1a, r1b, r2a, r2b, r3a, r3b, ua, ub, r4a, r4b,
    w_sem, a_send, a_recv, g_send, g_recv,
    s1_send, s1_recv, s2_send, s2_recv, s3_send, s3_recv, s4_send, s4_recv,
):
    me = lax.axis_index("wide")
    group = HEADS
    spot = lax.rem(me, group)
    base = me - spot
    depth = devices // 8
    core = lax.rem(me, 2)
    xi = lax.rem(me // 2, 2)
    yi = lax.rem(me // 4, 2)
    zi = me // 8
    n_q = q_ref.shape[0]
    width = v_ref.shape[1]
    patches = k_ref.shape[0]
    key_size = k_ref.shape[1] // HEADS
    value_size = width // HEADS
    extra = value_size - LANES
    pieces = LANES // extra
    half_w = width // 2
    rows_dev = re_ref.shape[1]
    wide_kv = kvp.shape[2]

    def dev(z, y, x, c):
        return z * 8 + y * 4 + x * 2 + c

    sib = dev(zi, yi, xi, 1 - core)
    xn = dev(zi, yi, 1 - xi, core)
    yn = dev(zi, 1 - yi, xi, core)

    def rcopy(src, dst, ssem, rsem, target):
        return pltpu.make_async_remote_copy(
            src_ref=src, dst_ref=dst, send_sem=ssem, recv_sem=rsem,
            device_id={"wide": target}, device_id_type=pl.DeviceIdType.MESH,
        )

    barrier = pltpu.get_barrier_semaphore()
    per_group = group // 8
    for k in range(1, group):
        pl.semaphore_signal(
            barrier, inc=1, device_id={"wide": base + lax.rem(spot + k, group)},
            device_id_type=pl.DeviceIdType.MESH,
        )
    far = depth - per_group
    z_base = zi // per_group * per_group
    for k in range(far):
        zt = lax.rem(z_base + per_group + k, depth)
        pl.semaphore_signal(
            barrier, inc=1, device_id={"wide": dev(zt, yi, xi, core)},
            device_id_type=pl.DeviceIdType.MESH,
        )

    w_copies = [
        pltpu.make_async_copy(wg_hbm, wg, w_sem.at[0]),
        pltpu.make_async_copy(wu_hbm, wu, w_sem.at[1]),
        pltpu.make_async_copy(wd_hbm, wd, w_sem.at[2]),
    ]
    in_copies = [
        pltpu.make_async_copy(k_hbm, k_ref, w_sem.at[3]),
        pltpu.make_async_copy(v_hbm, v_ref, w_sem.at[4]),
        pltpu.make_async_copy(q_hbm, q_ref, w_sem.at[5]),
    ]
    for c in in_copies:
        c.start()
    for c in in_copies:
        c.wait()

    pad = jnp.zeros((patches, wide_kv - value_size - key_size), BF16)
    for h in range(HEADS):
        kvp[h] = jnp.concatenate(
            [
                v_ref[:, h * value_size : (h + 1) * value_size],
                k_ref[:, h * key_size : (h + 1) * key_size],
                pad,
            ],
            axis=1,
        )
    pl.semaphore_wait(barrier, group - 1 + far)

    def a2a(k):
        t = lax.rem(spot + k, group)
        return rcopy(kvp.at[t], kvr.at[spot], a_send.at[k], a_recv.at[k], base + t)

    def a2a_in(k):
        s = lax.rem(spot + group - k, group)
        return rcopy(kvp.at[s], kvr.at[s], a_send.at[k], a_recv.at[k], base + s)

    def send_kv(k, carry):
        a2a(k).start()
        return carry

    lax.fori_loop(1, group, send_kv, 0)
    for c in w_copies:
        c.start()
    kvr[spot] = kvp[spot]

    q_head = jnp.zeros((n_q, key_size), F32)
    for h in range(HEADS):
        q_head = jnp.where(
            spot == h, q_ref[:, h * key_size : (h + 1) * key_size].astype(F32), q_head
        )
    q_pad = jnp.concatenate(
        [
            jnp.zeros((n_q, value_size), F32),
            q_head,
            jnp.zeros((n_q, wide_kv - value_size - key_size), F32),
        ],
        axis=1,
    ).astype(BF16)

    shares = rw_ref[...].astype(F32)
    shares = shares / jnp.sum(shares, axis=0, keepdims=True)
    split = LANES // 2
    line = lax.rem(lax.broadcasted_iota(jnp.int32, (LANES, rows_dev), 0), split)
    table = jnp.zeros((LANES, rows_dev), F32)
    for k in range(re_ref.shape[0]):
        table = table + jnp.where(re_ref[k : k + 1, :] == line, shares[k : k + 1, :], 0.0)
    table = jnp.concatenate([table, jnp.zeros((LANES, LANES - rows_dev), F32)], axis=1).T[:rows_dev]
    lane = lax.broadcasted_iota(jnp.int32, (rows_dev, LANES), 1)
    table_hi = table.astype(BF16).astype(F32)
    table = jnp.where(lane < split, table_hi, table - table_hi).astype(BF16)

    def wait_kv(k, carry):
        a2a_in(k).wait_recv()
        return carry

    lax.fori_loop(1, group, wait_kv, 0)

    scale = key_size ** (-0.5)
    for s in range(group):
        s_scr[:, s * patches : (s + 1) * patches] = (
            lax.dot_general(
                q_pad, kvr[s], (((1,), (1,)), ((), ())), preferred_element_type=F32
            )
            * scale
        )

    step = 32

    def soft(r, carry):
        rows = pl.ds(pl.multiple_of(r * step, step), step)
        s = s_scr[rows, :]
        p = jnp.exp(s - jnp.max(s, axis=1, keepdims=True))
        tot_scr[rows, :] = jnp.broadcast_to(jnp.sum(p, axis=1, keepdims=True), (step, LANES))
        p_scr[rows, :] = p.astype(BF16)
        return carry

    lax.fori_loop(0, n_q // step, soft, 0)
    acc = jnp.zeros((n_q, wide_kv), F32)
    for s in range(group):
        acc = acc + jnp.dot(
            p_scr[:, s * patches : (s + 1) * patches], kvr[s], preferred_element_type=F32
        )
    att = (acc / tot_scr[:, 0:1]).astype(BF16)
    main = n_q
    part = n_q // pieces
    gath[me, 0:main, :] = att[:, :LANES]
    gath[me, main : main + part, :] = jnp.concatenate(
        [att[g * part : (g + 1) * part, LANES : LANES + extra] for g in range(pieces)], axis=1
    )
    gath[me, main + part : main + part + rows_dev, :] = table

    tall = main + part + rows_dev
    half = tall // 32 * 16
    top, low = pl.ds(0, half), pl.ds(half, tall - half)

    def zo(i):
        near = z_base + lax.rem(lax.rem(zi, per_group) + i, per_group)
        return jnp.where(i < per_group, near, lax.rem(z_base + i, depth))

    def own(z):
        return dev(z, yi, xi, core)

    def blk_x(z):
        return dev(z, yi, 1 - xi, core)

    def blk_y(z):
        return dev(z, 1 - yi, xi, core)

    def blk_d(z):
        return dev(z, 1 - yi, 1 - xi, core)

    def gcopy(kind, z, block, target, rows=None):
        ref = gath.at[block] if rows is None else gath.at[block, rows]
        return rcopy(ref, ref, g_send.at[kind, z], g_recv.at[kind, z], target)

    def z_out(i):
        zt = zo(i)
        ref = gath.at[me]
        return rcopy(ref, ref, g_send.at[0, zt], g_recv.at[0, zi], own(zt))

    def send_z(i, carry):
        z_out(i).start()
        return carry

    lax.fori_loop(1, depth, send_z, 0)

    def spread(z):
        gcopy(1, z, own(z), xn).start()
        gcopy(2, z, own(z), yn).start()
        gcopy(3, z, own(z), sib).start()

    spread(zi)

    def spread_z(i, carry):
        gcopy(0, zo(i), own(zo(i)), own(zo(i))).wait_recv()
        spread(zo(i))
        return carry

    lax.fori_loop(1, per_group, spread_z, 0)

    def onward(i, carry):
        z = zo(i)
        gcopy(1, z, blk_x(z), xn).wait_recv()
        gcopy(4, z, blk_x(z), yn, top).start()
        gcopy(5, z, blk_x(z), sib).start()
        gcopy(2, z, blk_y(z), yn).wait_recv()
        gcopy(6, z, blk_y(z), xn, low).start()
        gcopy(7, z, blk_y(z), sib).start()
        return carry

    def last(i, carry):
        z = zo(i)
        gcopy(4, z, blk_d(z), yn, top).wait_recv()
        gcopy(6, z, blk_d(z), xn, low).wait_recv()
        gcopy(8, z, blk_d(z), sib).start()
        return carry

    def other(block):
        return block + 1 - 2 * core

    def from_sib(i, carry):
        z = zo(i)
        gcopy(3, z, other(own(z)), sib).wait_recv()
        gcopy(5, z, other(blk_x(z)), sib).wait_recv()
        gcopy(7, z, other(blk_y(z)), sib).wait_recv()
        gcopy(8, z, other(blk_d(z)), sib).wait_recv()
        return carry

    lax.fori_loop(0, per_group, onward, 0)
    lax.fori_loop(per_group, depth, spread_z, 0)
    lax.fori_loop(0, per_group, last, 0)
    lax.fori_loop(per_group, depth, onward, 0)

    images = devices // group
    quads = HEADS // pieces

    def lay(image, quad):
        first = image * group + quad * pieces
        cols = []
        for g in range(pieces):
            tail = gath[first + g, main : main + part, :]
            cols.append(gath[first + g, 0:main, :])
            cols.append(
                jnp.concatenate(
                    [tail[:, i * extra : (i + 1) * extra] for i in range(pieces)], axis=0
                )
            )
        span = pieces * value_size
        proj[
            pl.ds(pl.multiple_of(image * n_q, n_q), n_q),
            pl.ds(pl.multiple_of(quad * span, LANES), span),
        ] = jnp.concatenate(cols, axis=1)
    expert = me // 2
    lane_row = lax.rem(lane, split)

    def norm_rows(d, carry):
        rows = pl.ds(pl.multiple_of(d * rows_dev, rows_dev), rows_dev)
        x = proj[rows, :].astype(F32)
        r = lax.rsqrt(jnp.mean(x * x, axis=1, keepdims=True) + 1e-06)
        proj[rows, :] = (x * r * gain_ref[...].reshape(1, -1)).astype(BF16)
        share = gath[d, main + part : main + part + rows_dev, :].astype(F32)
        mine = jnp.sum(jnp.where(lane_row == expert, share, 0.0), axis=1, keepdims=True)
        gates[rows, :] = jnp.broadcast_to(mine, (rows_dev, LANES))
        return carry


    block_rows = n_q
    z_block = block_rows // (8 * rows_dev)

    def s1(z, side):
        src = pa if side == 0 else pb
        dst = r1a if side == 0 else r1b
        return rcopy(
            src.at[1 - core, :, z], dst.at[:, z], s1_send.at[side, z], s1_recv.at[side, z], sib
        )

    def experts(r):
        rows = pl.ds(pl.multiple_of(r * block_rows, block_rows), block_rows)
        x = proj[rows, :]
        dims = (((1,), (1,)), ((), ()))
        g = lax.dot_general(x, wg[...], dims, preferred_element_type=F32)
        u = lax.dot_general(x, wu[...], dims, preferred_element_type=F32)
        hidden = (g / (1.0 + jnp.exp(-g)) * u).astype(BF16)
        share = gates[rows, 0:1]
        chunk = half_w // 2
        for n in range(4):
            y = jnp.dot(
                hidden, wd[:, n * chunk : (n + 1) * chunk], preferred_element_type=F32
            )
            y = (y * share).astype(BF16)
            cols = slice((n % 2) * chunk, (n % 2 + 1) * chunk)
            for j in range(8 * z_block):
                c, x_, y_, z = j % 2, j // 2 % 2, j // 4 % 2, j // 8
                piece = y[j * rows_dev : (j + 1) * rows_dev]
                if n < 2:
                    pa[c, x_, r * z_block + z, y_, :, cols] = piece
                else:
                    pb[c, y_, r * z_block + z, x_, :, cols] = piece
        for z in range(z_block):
            s1(r * z_block + z, 0).start()
            s1(r * z_block + z, 1).start()

    def add_into(dst, d_ix, others):
        total = dst[d_ix].astype(F32)
        for ref, ix in others:
            total = total + ref[ix].astype(F32)
        return total.astype(BF16)

    def s2a(z):
        return rcopy(pa.at[core, 1 - xi, z], r2a.at[z], s2_send.at[0, z], s2_recv.at[0, z], xn)

    def s2b(z):
        return rcopy(pb.at[core, 1 - yi, z], r2b.at[z], s2_send.at[1, z], s2_recv.at[1, z], yn)

    def home1(i, carry):
        z = zo(i)
        s1(z, 0).wait_recv()
        pa[core, 1 - xi, z] = add_into(pa, (core, 1 - xi, z), [(r1a, (1 - xi, z))])
        s2a(z).start()
        s1(z, 1).wait_recv()
        pb[core, 1 - yi, z] = add_into(pb, (core, 1 - yi, z), [(r1b, (1 - yi, z))])
        s2b(z).start()
        return carry

    def s3a(z):
        return rcopy(
            pa.at[core, xi, z, 1 - yi], r3a.at[z], s3_send.at[0, z], s3_recv.at[0, z], yn
        )

    def s3b(z):
        return rcopy(
            pb.at[core, yi, z, 1 - xi], r3b.at[z], s3_send.at[1, z], s3_recv.at[1, z], xn
        )

    def home2(i, carry):
        z = zo(i)
        s2a(z).wait_recv()
        pa[core, xi, z] = add_into(pa, (core, xi, z), [(r1a, (xi, z)), (r2a, z)])
        s3a(z).start()
        s2b(z).wait_recv()
        pb[core, yi, z] = add_into(pb, (core, yi, z), [(r1b, (yi, z)), (r2b, z)])
        s3b(z).start()
        return carry

    def s4(zt, side):
        src = ua if side == 0 else ub
        dst = r4a if side == 0 else r4b
        return rcopy(
            src.at[zt], dst.at[zi], s4_send.at[side, zt], s4_recv.at[side, zi], own(zt)
        )

    def s4_in(z, side):
        dst = r4a if side == 0 else r4b
        return rcopy(
            dst.at[z], dst.at[z], s4_send.at[side, z], s4_recv.at[side, z], own(z)
        )

    def home3(i, carry):
        z = zo(i)
        s3a(z).wait_recv()
        ua[z] = add_into(pa, (core, xi, z, yi), [(r3a, z)])
        s3b(z).wait_recv()
        ub[z] = add_into(pb, (core, yi, z, xi), [(r3b, z)])

        @pl.when(i > 0)
        def _():
            s4(z, 0).start()
            s4(z, 1).start()

        return carry

    def each(i, carry):
        image = lax.rem(zi // per_group + i, images)
        first, end = per_group * i, per_group * (i + 1)

        @pl.when(i > 0)
        def _():
            lax.fori_loop(first, end, last, 0)
            lax.fori_loop(first - per_group, first, home1, 0)

        lax.fori_loop(first, end, from_sib, 0)

        def lay_quad(quad, c):
            lay(image, quad)
            return c

        lax.fori_loop(0, quads, lay_quad, 0)

        @pl.when(i == 0)
        def _():
            own_rows[...] = proj[pl.ds(pl.multiple_of(me * rows_dev, rows_dev), rows_dev), :]
            for c in w_copies:
                c.wait()

        lax.fori_loop(image * group, image * group + group, norm_rows, 0)

        @pl.when(i > 0)
        def _():
            lax.fori_loop(first - per_group, first, home2, 0)

        experts(image)

        @pl.when(i > 0)
        def _():
            lax.fori_loop(first - per_group, first, home3, 0)

        return carry

    lax.fori_loop(0, images, each, 0)
    for home in (home1, home2, home3):
        lax.fori_loop(depth - per_group, depth, home, 0)
    mine = own_rows[...].astype(F32)
    sum_a = mine[:, :half_w] + ua[zi].astype(F32)
    sum_b = mine[:, half_w:] + ub[zi].astype(F32)

    def home4(i, carry):
        left, right = carry
        z = zo(i)
        s4_in(z, 0).wait_recv()
        s4_in(z, 1).wait_recv()
        return left + r4a[z].astype(F32), right + r4b[z].astype(F32)

    sum_a, sum_b = lax.fori_loop(1, depth, home4, (sum_a, sum_b))
    out_ref[:, :half_w] = sum_a.astype(BF16)
    out_ref[:, half_w:] = sum_b.astype(BF16)

    def sent_kv(k, carry):
        a2a(k).wait_send()
        return carry

    lax.fori_loop(1, group, sent_kv, 0)

    def sent_z(i, carry):
        z_out(i).wait_send()
        s4(zo(i), 0).wait_send()
        s4(zo(i), 1).wait_send()
        return carry

    lax.fori_loop(1, depth, sent_z, 0)

    def sent(dz, carry):
        gcopy(1, dz, own(dz), xn).wait_send()
        gcopy(2, dz, own(dz), yn).wait_send()
        gcopy(3, dz, own(dz), sib).wait_send()
        gcopy(4, dz, blk_x(dz), yn, top).wait_send()
        gcopy(5, dz, blk_x(dz), sib).wait_send()
        gcopy(6, dz, blk_y(dz), xn, low).wait_send()
        gcopy(7, dz, blk_y(dz), sib).wait_send()
        gcopy(8, dz, blk_d(dz), sib).wait_send()
        for copy in (s1(dz, 0), s1(dz, 1), s2a(dz), s2b(dz), s3a(dz), s3b(dz)):
            copy.wait_send()
        return carry

    lax.fori_loop(0, depth, sent, 0)


def on_device(
    queries, patch_keys, patch_values, norm_gain, route_experts, route_weights, w_gate, w_up, w_down
):
    devices = lax.axis_size("wide")
    n_q = queries.shape[0]
    patches, vision = patch_keys.shape
    width = patch_values.shape[1]
    rows_dev = route_experts.shape[0]
    assert devices // 2 <= LANES // 2
    hidden = w_gate.shape[0]
    depth = devices // 8
    group = HEADS
    assert n_q == rows_dev * group and n_q % (8 * rows_dev) == 0 and depth % 2 == 0
    value_size = width // HEADS
    extra = value_size - LANES
    pieces = LANES // extra
    wide_kv = -(-(value_size + vision // HEADS) // LANES) * LANES
    tall = n_q + n_q // pieces + rows_dev
    rows = devices * rows_dev
    half = width // 2
    vm = pltpu.VMEM
    dma = pltpu.SemaphoreType.DMA
    scratch = [
        vm(queries.shape, BF16),
        vm(patch_keys.shape, BF16),
        vm(patch_values.shape, BF16),
        vm((group, patches, wide_kv), BF16),
        vm((group, patches, wide_kv), BF16),
        vm((n_q, group * patches), F32),
        vm((n_q, group * patches), BF16),
        vm((n_q, LANES), F32),
        vm((devices, tall, LANES), BF16),
        vm((rows, width), BF16),
        vm((rows_dev, width), BF16),
        vm((rows, LANES), F32),
        vm((hidden, width), BF16),
        vm((hidden, width), BF16),
        vm((hidden, width), BF16),
        vm((2, 2, depth, 2, rows_dev, half), BF16),
        vm((2, 2, depth, 2, rows_dev, half), BF16),
        vm((2, depth, 2, rows_dev, half), BF16),
        vm((2, depth, 2, rows_dev, half), BF16),
        vm((depth, 2, rows_dev, half), BF16),
        vm((depth, 2, rows_dev, half), BF16),
        vm((depth, rows_dev, half), BF16),
        vm((depth, rows_dev, half), BF16),
        vm((depth, rows_dev, half), BF16),
        vm((depth, rows_dev, half), BF16),
        vm((depth, rows_dev, half), BF16),
        vm((depth, rows_dev, half), BF16),
        dma((6,)),
        dma((group,)), dma((group,)),
        dma((9, depth)), dma((9, depth)),
        dma((2, depth)), dma((2, depth)),
        dma((2, depth)), dma((2, depth)),
        dma((2, depth)), dma((2, depth)),
        dma((2, depth)), dma((2, depth)),
    ]
    vspec = pl.BlockSpec(memory_space=pltpu.VMEM)
    hspec = pl.BlockSpec(memory_space=pl.ANY)
    return pl.pallas_call(
        functools.partial(kernel, devices),
        out_shape=jax.ShapeDtypeStruct((rows_dev, width), BF16),
        in_specs=[hspec] * 3 + [vspec] * 3 + [hspec] * 3,
        out_specs=vspec,
        scratch_shapes=scratch,
        compiler_params=pltpu.CompilerParams(
            collective_id=0, has_side_effects=True, vmem_limit_bytes=62 * 1024 * 1024
        ),
    )(
        queries, patch_keys, patch_values, norm_gain, route_experts.T, route_weights.T,
        w_gate, w_up, w_down,
    )


def solution(mesh):
    rows = P(("groups", "wide"), None)
    return jax.shard_map(
        on_device,
        mesh=mesh,
        in_specs=(
            P("groups", None), rows, rows, P(), rows, rows,
            P("wide", None), P("wide", None), P("wide", None),
        ),
        out_specs=rows,
        check_vma=False,
    )
```

```python
import functools

import jax
import jax.numpy as jnp
from jax import lax
from jax.experimental import pallas as pl
from jax.experimental.pallas import tpu as pltpu
from jax.sharding import PartitionSpec as P

HEADS = 16
LANES = 128
F32 = jnp.float32
BF16 = jnp.bfloat16


def kernel(
    devices,
    q_hbm, k_hbm, v_hbm, gain_ref, re_ref, rw_ref, wg_hbm, wu_hbm, wd_hbm,
    out_ref,
    q_ref, k_ref, v_ref, kvp, kvr, s_scr, p_scr, tot_scr, gath, proj, own_rows, gates, wg, wu, wd,
    pa, pb, r1a, r1b, r2a, r2b, r3a, r3b, ua, ub, r4a, r4b,
    w_sem, a_send, a_recv, g_send, g_recv,
    s1_send, s1_recv, s2_send, s2_recv, s3_send, s3_recv, s4_send, s4_recv,
):
    me = lax.axis_index("wide")
    group = HEADS
    spot = lax.rem(me, group)
    base = me - spot
    depth = devices // 8
    core = lax.rem(me, 2)
    xi = lax.rem(me // 2, 2)
    yi = lax.rem(me // 4, 2)
    zi = me // 8
    n_q = q_ref.shape[0]
    width = v_ref.shape[1]
    patches = k_ref.shape[0]
    key_size = k_ref.shape[1] // HEADS
    value_size = width // HEADS
    extra = value_size - LANES
    pieces = LANES // extra
    half_w = width // 2
    rows_dev = re_ref.shape[1]
    wide_kv = kvp.shape[2]

    def dev(z, y, x, c):
        return z * 8 + y * 4 + x * 2 + c

    sib = dev(zi, yi, xi, 1 - core)
    xn = dev(zi, yi, 1 - xi, core)
    yn = dev(zi, 1 - yi, xi, core)

    def rcopy(src, dst, ssem, rsem, target):
        return pltpu.make_async_remote_copy(
            src_ref=src, dst_ref=dst, send_sem=ssem, recv_sem=rsem,
            device_id={"wide": target}, device_id_type=pl.DeviceIdType.MESH,
        )

    barrier = pltpu.get_barrier_semaphore()
    per_group = group // 8
    for k in range(1, group):
        pl.semaphore_signal(
            barrier, inc=1, device_id={"wide": base + lax.rem(spot + k, group)},
            device_id_type=pl.DeviceIdType.MESH,
        )
    far = depth - per_group
    z_base = zi // per_group * per_group
    for k in range(far):
        zt = lax.rem(z_base + per_group + k, depth)
        pl.semaphore_signal(
            barrier, inc=1, device_id={"wide": dev(zt, yi, xi, core)},
            device_id_type=pl.DeviceIdType.MESH,
        )

    w_copies = [
        pltpu.make_async_copy(wg_hbm, wg, w_sem.at[0]),
        pltpu.make_async_copy(wu_hbm, wu, w_sem.at[1]),
        pltpu.make_async_copy(wd_hbm, wd, w_sem.at[2]),
    ]
    in_copies = [
        pltpu.make_async_copy(k_hbm, k_ref, w_sem.at[3]),
        pltpu.make_async_copy(v_hbm, v_ref, w_sem.at[4]),
        pltpu.make_async_copy(q_hbm, q_ref, w_sem.at[5]),
    ]
    for c in in_copies:
        c.start()
    for c in in_copies:
        c.wait()

    pad = jnp.zeros((patches, wide_kv - value_size - key_size), BF16)
    for h in range(HEADS):
        kvp[h] = jnp.concatenate(
            [
                v_ref[:, h * value_size : (h + 1) * value_size],
                k_ref[:, h * key_size : (h + 1) * key_size],
                pad,
            ],
            axis=1,
        )
    pl.semaphore_wait(barrier, group - 1 + far)

    def a2a(k):
        t = lax.rem(spot + k, group)
        return rcopy(kvp.at[t], kvr.at[spot], a_send.at[k], a_recv.at[k], base + t)

    def a2a_in(k):
        s = lax.rem(spot + group - k, group)
        return rcopy(kvp.at[s], kvr.at[s], a_send.at[k], a_recv.at[k], base + s)

    def send_kv(k, carry):
        a2a(k).start()
        return carry

    lax.fori_loop(1, group, send_kv, 0)
    for c in w_copies:
        c.start()
    kvr[spot] = kvp[spot]

    q_head = jnp.zeros((n_q, key_size), F32)
    for h in range(HEADS):
        q_head = jnp.where(
            spot == h, q_ref[:, h * key_size : (h + 1) * key_size].astype(F32), q_head
        )
    q_pad = jnp.concatenate(
        [
            jnp.zeros((n_q, value_size), F32),
            q_head,
            jnp.zeros((n_q, wide_kv - value_size - key_size), F32),
        ],
        axis=1,
    ).astype(BF16)

    shares = rw_ref[...].astype(F32)
    shares = shares / jnp.sum(shares, axis=0, keepdims=True)
    split = LANES // 2
    line = lax.rem(lax.broadcasted_iota(jnp.int32, (LANES, rows_dev), 0), split)
    table = jnp.zeros((LANES, rows_dev), F32)
    for k in range(re_ref.shape[0]):
        table = table + jnp.where(re_ref[k : k + 1, :] == line, shares[k : k + 1, :], 0.0)
    table = jnp.concatenate([table, jnp.zeros((LANES, LANES - rows_dev), F32)], axis=1).T[:rows_dev]
    lane = lax.broadcasted_iota(jnp.int32, (rows_dev, LANES), 1)
    table_hi = table.astype(BF16).astype(F32)
    table = jnp.where(lane < split, table_hi, table - table_hi).astype(BF16)

    scale = key_size ** (-0.5)
    for k in range(group):
        if k > 0:
            a2a_in(k).wait_recv()
        s_scr[:, k * patches : (k + 1) * patches] = (
            lax.dot_general(
                q_pad, kvr[lax.rem(spot + group - k, group)], (((1,), (1,)), ((), ())),
                preferred_element_type=F32,
            )
            * scale
        )

    step = 32

    def soft(r, carry):
        rows = pl.ds(pl.multiple_of(r * step, step), step)
        s = s_scr[rows, :]
        p = jnp.exp(s - jnp.max(s, axis=1, keepdims=True))
        tot_scr[rows, :] = jnp.broadcast_to(jnp.sum(p, axis=1, keepdims=True), (step, LANES))
        p_scr[rows, :] = p.astype(BF16)
        return carry

    lax.fori_loop(0, n_q // step, soft, 0)
    acc = jnp.zeros((n_q, wide_kv), F32)
    for s in range(group):
        acc = acc + jnp.dot(
            p_scr[:, s * patches : (s + 1) * patches],
            kvr[lax.rem(spot + group - s, group)],
            preferred_element_type=F32,
        )
    att = (acc / tot_scr[:, 0:1]).astype(BF16)
    main = n_q
    part = n_q // pieces
    gath[me, 0:main, :] = att[:, :LANES]
    gath[me, main : main + part, :] = jnp.concatenate(
        [att[g * part : (g + 1) * part, LANES : LANES + extra] for g in range(pieces)], axis=1
    )
    gath[me, main + part : main + part + rows_dev, :] = table

    tall = main + part + rows_dev
    half = tall // 32 * 16
    top, low = pl.ds(0, half), pl.ds(half, tall - half)

    def zo(i):
        near = z_base + lax.rem(lax.rem(zi, per_group) + i, per_group)
        return jnp.where(i < per_group, near, lax.rem(z_base + i, depth))

    def own(z):
        return dev(z, yi, xi, core)

    def blk_x(z):
        return dev(z, yi, 1 - xi, core)

    def blk_y(z):
        return dev(z, 1 - yi, xi, core)

    def blk_d(z):
        return dev(z, 1 - yi, 1 - xi, core)

    def gcopy(kind, z, block, target, rows=None):
        ref = gath.at[block] if rows is None else gath.at[block, rows]
        return rcopy(ref, ref, g_send.at[kind, z], g_recv.at[kind, z], target)

    def z_out(i):
        zt = zo(i)
        ref = gath.at[me]
        return rcopy(ref, ref, g_send.at[0, zt], g_recv.at[0, zi], own(zt))

    def send_z(i, carry):
        z_out(i).start()
        return carry

    lax.fori_loop(1, depth, send_z, 0)

    def spread(z):
        gcopy(1, z, own(z), xn).start()
        gcopy(2, z, own(z), yn).start()
        gcopy(3, z, own(z), sib).start()

    spread(zi)

    def spread_z(i, carry):
        gcopy(0, zo(i), own(zo(i)), own(zo(i))).wait_recv()
        spread(zo(i))
        return carry

    lax.fori_loop(1, per_group, spread_z, 0)

    def onward(i, carry):
        z = zo(i)
        gcopy(1, z, blk_x(z), xn).wait_recv()
        gcopy(4, z, blk_x(z), yn, top).start()
        gcopy(5, z, blk_x(z), sib).start()
        gcopy(2, z, blk_y(z), yn).wait_recv()
        gcopy(6, z, blk_y(z), xn, low).start()
        gcopy(7, z, blk_y(z), sib).start()
        return carry

    def last(i, carry):
        z = zo(i)
        gcopy(4, z, blk_d(z), yn, top).wait_recv()
        gcopy(6, z, blk_d(z), xn, low).wait_recv()
        gcopy(8, z, blk_d(z), sib).start()
        return carry

    def other(block):
        return block + 1 - 2 * core

    def from_sib(i, carry):
        z = zo(i)
        gcopy(3, z, other(own(z)), sib).wait_recv()
        gcopy(5, z, other(blk_x(z)), sib).wait_recv()
        gcopy(7, z, other(blk_y(z)), sib).wait_recv()
        gcopy(8, z, other(blk_d(z)), sib).wait_recv()
        return carry

    lax.fori_loop(0, per_group, onward, 0)
    lax.fori_loop(per_group, depth, spread_z, 0)
    lax.fori_loop(0, per_group, last, 0)
    lax.fori_loop(per_group, depth, onward, 0)

    images = devices // group
    quads = HEADS // pieces

    def lay(image, quad):
        first = image * group + quad * pieces
        cols = []
        for g in range(pieces):
            tail = gath[first + g, main : main + part, :]
            cols.append(gath[first + g, 0:main, :])
            cols.append(
                jnp.concatenate(
                    [tail[:, i * extra : (i + 1) * extra] for i in range(pieces)], axis=0
                )
            )
        span = pieces * value_size
        proj[
            pl.ds(pl.multiple_of(image * n_q, n_q), n_q),
            pl.ds(pl.multiple_of(quad * span, LANES), span),
        ] = jnp.concatenate(cols, axis=1)
    expert = me // 2
    lane_row = lax.rem(lane, split)

    def norm_rows(d, carry):
        rows = pl.ds(pl.multiple_of(d * rows_dev, rows_dev), rows_dev)
        x = proj[rows, :].astype(F32)
        r = lax.rsqrt(jnp.mean(x * x, axis=1, keepdims=True) + 1e-06)
        proj[rows, :] = (x * r * gain_ref[...].reshape(1, -1)).astype(BF16)
        share = gath[d, main + part : main + part + rows_dev, :].astype(F32)
        mine = jnp.sum(jnp.where(lane_row == expert, share, 0.0), axis=1, keepdims=True)
        gates[rows, :] = jnp.broadcast_to(mine, (rows_dev, LANES))
        return carry


    block_rows = n_q
    z_block = block_rows // (8 * rows_dev)

    def s1(z, side):
        src = pa if side == 0 else pb
        dst = r1a if side == 0 else r1b
        return rcopy(
            src.at[1 - core, :, z], dst.at[:, z], s1_send.at[side, z], s1_recv.at[side, z], sib
        )

    def experts(r):
        rows = pl.ds(pl.multiple_of(r * block_rows, block_rows), block_rows)
        x = proj[rows, :]
        dims = (((1,), (1,)), ((), ()))
        g = lax.dot_general(x, wg[...], dims, preferred_element_type=F32)
        u = lax.dot_general(x, wu[...], dims, preferred_element_type=F32)
        hidden = (g / (1.0 + jnp.exp(-g)) * u).astype(BF16)
        share = gates[rows, 0:1]
        chunk = half_w // 2
        for n in range(4):
            y = jnp.dot(
                hidden, wd[:, n * chunk : (n + 1) * chunk], preferred_element_type=F32
            )
            y = (y * share).astype(BF16)
            cols = slice((n % 2) * chunk, (n % 2 + 1) * chunk)
            for j in range(8 * z_block):
                c, x_, y_, z = j % 2, j // 2 % 2, j // 4 % 2, j // 8
                piece = y[j * rows_dev : (j + 1) * rows_dev]
                if n < 2:
                    pa[c, x_, r * z_block + z, y_, :, cols] = piece
                else:
                    pb[c, y_, r * z_block + z, x_, :, cols] = piece
        for z in range(z_block):
            s1(r * z_block + z, 0).start()
            s1(r * z_block + z, 1).start()

    def add_into(dst, d_ix, others):
        total = dst[d_ix].astype(F32)
        for ref, ix in others:
            total = total + ref[ix].astype(F32)
        return total.astype(BF16)

    def s2a(z):
        return rcopy(pa.at[core, 1 - xi, z], r2a.at[z], s2_send.at[0, z], s2_recv.at[0, z], xn)

    def s2b(z):
        return rcopy(pb.at[core, 1 - yi, z], r2b.at[z], s2_send.at[1, z], s2_recv.at[1, z], yn)

    def home1(i, carry):
        z = zo(i)
        s1(z, 0).wait_recv()
        pa[core, 1 - xi, z] = add_into(pa, (core, 1 - xi, z), [(r1a, (1 - xi, z))])
        s2a(z).start()
        s1(z, 1).wait_recv()
        pb[core, 1 - yi, z] = add_into(pb, (core, 1 - yi, z), [(r1b, (1 - yi, z))])
        s2b(z).start()
        return carry

    def s3a(z):
        return rcopy(
            pa.at[core, xi, z, 1 - yi], r3a.at[z], s3_send.at[0, z], s3_recv.at[0, z], yn
        )

    def s3b(z):
        return rcopy(
            pb.at[core, yi, z, 1 - xi], r3b.at[z], s3_send.at[1, z], s3_recv.at[1, z], xn
        )

    def home2(i, carry):
        z = zo(i)
        s2a(z).wait_recv()
        pa[core, xi, z] = add_into(pa, (core, xi, z), [(r1a, (xi, z)), (r2a, z)])
        s3a(z).start()
        s2b(z).wait_recv()
        pb[core, yi, z] = add_into(pb, (core, yi, z), [(r1b, (yi, z)), (r2b, z)])
        s3b(z).start()
        return carry

    def s4(zt, side):
        src = ua if side == 0 else ub
        dst = r4a if side == 0 else r4b
        return rcopy(
            src.at[zt], dst.at[zi], s4_send.at[side, zt], s4_recv.at[side, zi], own(zt)
        )

    def s4_in(z, side):
        dst = r4a if side == 0 else r4b
        return rcopy(
            dst.at[z], dst.at[z], s4_send.at[side, z], s4_recv.at[side, z], own(z)
        )

    def home3(i, carry):
        z = zo(i)
        s3a(z).wait_recv()
        ua[z] = add_into(pa, (core, xi, z, yi), [(r3a, z)])
        s3b(z).wait_recv()
        ub[z] = add_into(pb, (core, yi, z, xi), [(r3b, z)])

        @pl.when(i > 0)
        def _():
            s4(z, 0).start()
            s4(z, 1).start()

        return carry

    def each(i, carry):
        image = lax.rem(zi // per_group + i, images)
        first, end = per_group * i, per_group * (i + 1)

        @pl.when(i > 0)
        def _():
            lax.fori_loop(first, end, last, 0)
            lax.fori_loop(first - per_group, first, home1, 0)

        lax.fori_loop(first, end, from_sib, 0)

        def lay_quad(quad, c):
            lay(image, quad)
            return c

        lax.fori_loop(0, quads, lay_quad, 0)

        @pl.when(i == 0)
        def _():
            own_rows[...] = proj[pl.ds(pl.multiple_of(me * rows_dev, rows_dev), rows_dev), :]
            for c in w_copies:
                c.wait()

        lax.fori_loop(image * group, image * group + group, norm_rows, 0)

        @pl.when(i > 0)
        def _():
            lax.fori_loop(first - per_group, first, home2, 0)

        experts(image)

        @pl.when(i > 0)
        def _():
            lax.fori_loop(first - per_group, first, home3, 0)

        return carry

    lax.fori_loop(0, images, each, 0)
    for home in (home1, home2, home3):
        lax.fori_loop(depth - per_group, depth, home, 0)
    mine = own_rows[...].astype(F32)
    sum_a = mine[:, :half_w] + ua[zi].astype(F32)
    sum_b = mine[:, half_w:] + ub[zi].astype(F32)

    def home4(i, carry):
        left, right = carry
        z = zo(i)
        s4_in(z, 0).wait_recv()
        s4_in(z, 1).wait_recv()
        return left + r4a[z].astype(F32), right + r4b[z].astype(F32)

    sum_a, sum_b = lax.fori_loop(1, depth, home4, (sum_a, sum_b))
    out_ref[:, :half_w] = sum_a.astype(BF16)
    out_ref[:, half_w:] = sum_b.astype(BF16)

    def sent_kv(k, carry):
        a2a(k).wait_send()
        return carry

    lax.fori_loop(1, group, sent_kv, 0)

    def sent_z(i, carry):
        z_out(i).wait_send()
        s4(zo(i), 0).wait_send()
        s4(zo(i), 1).wait_send()
        return carry

    lax.fori_loop(1, depth, sent_z, 0)

    def sent(dz, carry):
        gcopy(1, dz, own(dz), xn).wait_send()
        gcopy(2, dz, own(dz), yn).wait_send()
        gcopy(3, dz, own(dz), sib).wait_send()
        gcopy(4, dz, blk_x(dz), yn, top).wait_send()
        gcopy(5, dz, blk_x(dz), sib).wait_send()
        gcopy(6, dz, blk_y(dz), xn, low).wait_send()
        gcopy(7, dz, blk_y(dz), sib).wait_send()
        gcopy(8, dz, blk_d(dz), sib).wait_send()
        for copy in (s1(dz, 0), s1(dz, 1), s2a(dz), s2b(dz), s3a(dz), s3b(dz)):
            copy.wait_send()
        return carry

    lax.fori_loop(0, depth, sent, 0)


def on_device(
    queries, patch_keys, patch_values, norm_gain, route_experts, route_weights, w_gate, w_up, w_down
):
    devices = lax.axis_size("wide")
    n_q = queries.shape[0]
    patches, vision = patch_keys.shape
    width = patch_values.shape[1]
    rows_dev = route_experts.shape[0]
    assert devices // 2 <= LANES // 2
    hidden = w_gate.shape[0]
    depth = devices // 8
    group = HEADS
    assert n_q == rows_dev * group and n_q % (8 * rows_dev) == 0 and depth % 2 == 0
    value_size = width // HEADS
    extra = value_size - LANES
    pieces = LANES // extra
    wide_kv = -(-(value_size + vision // HEADS) // LANES) * LANES
    tall = n_q + n_q // pieces + rows_dev
    rows = devices * rows_dev
    half = width // 2
    vm = pltpu.VMEM
    dma = pltpu.SemaphoreType.DMA
    scratch = [
        vm(queries.shape, BF16),
        vm(patch_keys.shape, BF16),
        vm(patch_values.shape, BF16),
        vm((group, patches, wide_kv), BF16),
        vm((group, patches, wide_kv), BF16),
        vm((n_q, group * patches), F32),
        vm((n_q, group * patches), BF16),
        vm((n_q, LANES), F32),
        vm((devices, tall, LANES), BF16),
        vm((rows, width), BF16),
        vm((rows_dev, width), BF16),
        vm((rows, LANES), F32),
        vm((hidden, width), BF16),
        vm((hidden, width), BF16),
        vm((hidden, width), BF16),
        vm((2, 2, depth, 2, rows_dev, half), BF16),
        vm((2, 2, depth, 2, rows_dev, half), BF16),
        vm((2, depth, 2, rows_dev, half), BF16),
        vm((2, depth, 2, rows_dev, half), BF16),
        vm((depth, 2, rows_dev, half), BF16),
        vm((depth, 2, rows_dev, half), BF16),
        vm((depth, rows_dev, half), BF16),
        vm((depth, rows_dev, half), BF16),
        vm((depth, rows_dev, half), BF16),
        vm((depth, rows_dev, half), BF16),
        vm((depth, rows_dev, half), BF16),
        vm((depth, rows_dev, half), BF16),
        dma((6,)),
        dma((group,)), dma((group,)),
        dma((9, depth)), dma((9, depth)),
        dma((2, depth)), dma((2, depth)),
        dma((2, depth)), dma((2, depth)),
        dma((2, depth)), dma((2, depth)),
        dma((2, depth)), dma((2, depth)),
    ]
    vspec = pl.BlockSpec(memory_space=pltpu.VMEM)
    hspec = pl.BlockSpec(memory_space=pl.ANY)
    return pl.pallas_call(
        functools.partial(kernel, devices),
        out_shape=jax.ShapeDtypeStruct((rows_dev, width), BF16),
        in_specs=[hspec] * 3 + [vspec] * 3 + [hspec] * 3,
        out_specs=vspec,
        scratch_shapes=scratch,
        compiler_params=pltpu.CompilerParams(
            collective_id=0, has_side_effects=True, vmem_limit_bytes=62 * 1024 * 1024
        ),
    )(
        queries, patch_keys, patch_values, norm_gain, route_experts.T, route_weights.T,
        w_gate, w_up, w_down,
    )


def solution(mesh):
    rows = P(("groups", "wide"), None)
    return jax.shard_map(
        on_device,
        mesh=mesh,
        in_specs=(
            P("groups", None), rows, rows, P(), rows, rows,
            P("wide", None), P("wide", None), P("wide", None),
        ),
        out_specs=rows,
        check_vma=False,
    )
```
